32 devices in a mesh: band: 2 (over x), stn: 8 (over z, y), tm: 2 (over core).
Axes of the slice: x: 2, y: 2, z: 4, core: 2. Of those that a mesh axis runs over, the one named last changes fastest.
Arguments:
- voltages: int32 [704, 4, 32768], P('stn', 'band', 'tm'), parts along dimension 1, may hold values from -125 to 125, as said below
- filter_taps: float32 [16, 128], replicated, may hold values from -0.036 to 0.036
Outputs:
- visibilities: float32 [2, 2, 128, 704, 704], P(None, None, ('band', 'stn', 'tm')), parts along dimension 2
The draws below stay inside these ranges and needn't reach their ends.
There are 2 independent parts, one for each index of `band`. The reference program is written for one: setup_inputs(seed, part) draws one part's arguments, and reference() takes and returns one part's arrays. A program takes and returns all parts, laid end to end along the dimension named above; an argument that names none is the same for every part. Nothing has to cross between parts.
Inputs may be any that keep to these rules, and one draw needn't show every extreme that they name: `voltages`: each input's samples are an integer gain of -2 to 2 times a signal common to all inputs plus noise of its own.
All inputs are finite; a program needn't handle non-finite values.
Results may differ from the reference program's by a relative error of at most 0.00049.
Values may be sent and summed in bfloat16 or wider, within the bound.
A program may use at most 192 MiB of HBM per device.

```python
import math
import jax
import jax.numpy as jnp
from jax import lax

INPUTS = 704
CH = 64
TAPS = 16
INTEG = 2
SPECTRA = 256
FRAME = 128
TIME = 32768


def draw_voltages(key, part):
    common_key = jax.random.fold_in(key, 11)
    gain_key = jax.random.fold_in(key, 23)
    noise_key = jax.random.fold_in(key, 37)
    common = jax.random.randint(common_key, (INTEG, TIME), -40, 41, dtype=jnp.int32)
    gains = jax.random.randint(gain_key, (INPUTS, 1, 1), -2, 3, dtype=jnp.int32)
    noise = jax.random.randint(noise_key, (INPUTS, INTEG, TIME), -45, 46, dtype=jnp.int32)
    return gains * common[None] + noise


def gaussian(rng, shape, deviation, reach, kind=jnp.bfloat16):
    return jnp.clip(deviation * jax.random.normal(rng, shape, jnp.float32), -reach, reach).astype(kind)


def setup_inputs(seed: int = 0, part: int = 0) -> dict:
    arg_keys = jax.random.split(jax.random.key(seed), 3)
    part_keys = jax.random.split(jax.random.fold_in(arg_keys[2], part), 3)
    voltages = draw_voltages(jax.random.fold_in(jax.random.fold_in(arg_keys[2], part), 71), part)
    filter_taps = gaussian(arg_keys[1], (TAPS, FRAME), 0.006, 0.036, jnp.float32)
    return {"voltages": voltages, "filter_taps": filter_taps}


def transform_table(frame_len, chan_count):
    sample_index = jnp.arange(frame_len, dtype=jnp.int32)[:, None]
    chan_index = jnp.arange(chan_count, dtype=jnp.int32)[None, :]
    phase = (2 * chan_index + 1) * sample_index % (2 * frame_len)
    angle = phase.astype(jnp.float32) * (math.pi / frame_len)
    factor = 1.0 / math.sqrt(frame_len)
    cosine = jnp.cos(angle) * factor
    sine = -jnp.sin(angle) * factor
    return jnp.stack([cosine, sine], axis=2).reshape(frame_len, 2 * chan_count)

def reference(voltages, filter_taps):
    total = INTEG * SPECTRA
    stream = voltages.astype(jnp.float32).reshape(INPUTS, total, FRAME)
    padded = jnp.concatenate([jnp.zeros((INPUTS, TAPS - 1, FRAME), jnp.float32), stream], axis=1)
    filtered = filter_taps[0] * padded[:, 0:total]
    for tap_index in range(1, TAPS):
        filtered = filtered + filter_taps[tap_index] * padded[:, tap_index:tap_index + total]
    table = transform_table(FRAME, CH)
    spectra = jnp.dot(filtered.reshape(-1, FRAME), table, precision=lax.Precision.HIGHEST, preferred_element_type=jnp.float32).astype(jnp.bfloat16)
    spectra = spectra.reshape(INPUTS, INTEG, SPECTRA, 2 * CH)

    def one_channel(index):
        pair = lax.dynamic_slice_in_dim(spectra, (2 * index).astype(jnp.int32), 2, axis=3)
        stacked = jnp.transpose(pair, (1, 3, 0, 2)).reshape(INTEG, 2 * INPUTS, SPECTRA).astype(jnp.float32)
        blocks = jnp.einsum('gas,gbs->gab', stacked, stacked, precision=lax.Precision.HIGHEST)
        blocks = blocks.reshape(INTEG, 2, INPUTS, 2, INPUTS)
        real_part = blocks[:, 0, :, 0] + blocks[:, 1, :, 1]
        imag_part = blocks[:, 1, :, 0] - blocks[:, 0, :, 1]
        return jnp.stack([real_part, imag_part]) * (1.0 / SPECTRA)
    result = lax.map(one_channel, jnp.arange(CH, dtype=jnp.int32))
    return jnp.transpose(result, (1, 2, 0, 3, 4))
```

```python
import functools
import math

import jax
import jax.numpy as jnp
import numpy as np
from jax import lax
from jax.experimental import pallas as pl
from jax.experimental.pallas import tpu as pltpu
from jax.sharding import PartitionSpec as P

MESH = pl.DeviceIdType.MESH
ROWS = 8


def passed_along(value, axis, steps):
    count = lax.axis_size(axis)
    pairs = [(source, (source + steps) % count) for source in range(count)]
    return lax.ppermute(value, axis, pairs)


def transform_table(frame_len, chan_count):
    sample_index = np.arange(frame_len)[:, None]
    chan_index = np.arange(chan_count)[None, :]
    phase = (2 * chan_index + 1) * sample_index % (2 * frame_len)
    angle = phase.astype(np.float64) * (math.pi / frame_len)
    factor = 1.0 / math.sqrt(frame_len)
    cosine = np.cos(angle) * factor
    sine = -np.sin(angle) * factor
    table = np.stack([cosine, sine], axis=2).reshape(frame_len, 2 * chan_count)
    return table.astype(np.float32)


def arrange(blocks):
    stations, blocks_time, per_dev, parts_two, inputs_dev, sub_count, spec_dev = blocks.shape
    ordered = jnp.transpose(blocks, (3, 5, 2, 0, 4, 1, 6))
    return ordered.reshape(
        parts_two, sub_count, per_dev, stations * inputs_dev, blocks_time * spec_dev
    )


def correlate(stacked):
    real_in = stacked[0]
    imag_in = stacked[1]
    right_side = jnp.concatenate([real_in, imag_in], axis=-1)
    left_imag = jnp.concatenate([imag_in, -real_in], axis=-1)
    real_part = jnp.einsum(
        "gcis,gcjs->gcij", right_side, right_side, preferred_element_type=jnp.float32
    )
    imag_part = jnp.einsum(
        "gcis,gcjs->gcij", left_imag, right_side, preferred_element_type=jnp.float32
    )
    return jnp.stack([real_part, imag_part])


def general_shards(voltages, filter_taps):
    inputs_dev, sub_count, time_dev = voltages.shape
    taps_count, frame_len = filter_taps.shape
    spec_dev = time_dev // frame_len
    chan_count = frame_len // 2
    lagging = taps_count - 1
    frames = voltages.astype(jnp.bfloat16).reshape(inputs_dev, sub_count, spec_dev, frame_len)
    last_frames = frames[:, :, spec_dev - lagging :, :]
    received = passed_along(last_frames, "tm", 1)
    earlier = jnp.concatenate([jnp.zeros_like(received[:, :1]), received[:, :-1]], axis=1)
    history = jnp.where(lax.axis_index("tm") == 0, earlier, received)
    extended = jnp.concatenate([history, frames], axis=2).astype(jnp.float32)
    filtered = filter_taps[0] * extended[:, :, 0:spec_dev]
    for tap_index in range(1, taps_count):
        filtered = (
            filtered + filter_taps[tap_index] * extended[:, :, tap_index : tap_index + spec_dev]
        )
    table = jnp.asarray(transform_table(frame_len, chan_count))
    spectra = lax.dot_general(
        table,
        filtered.reshape(-1, frame_len),
        (((0,), (1,)), ((), ())),
        precision=lax.Precision.HIGHEST,
        preferred_element_type=jnp.float32,
    ).astype(jnp.bfloat16)
    stations = lax.axis_size("stn")
    halves = lax.axis_size("tm")
    scale = 1.0 / (spec_dev * halves)
    moved = lax.all_to_all(spectra[None], ("stn", "tm"), split_axis=1, concat_axis=0, tiled=True)
    per_dev = moved.shape[1] // 2
    blocks = moved.reshape(stations, halves, per_dev, 2, inputs_dev, sub_count, spec_dev)
    result = correlate(arrange(blocks))
    return result * scale


def flipped(index, mask, count):
    total = 0
    bit = 1
    while bit < count:
        value = (index // bit) % 2
        total = total + (1 - value if mask & bit else value) * bit
        bit *= 2
    return total


def spectra_kernel(
    group, x_ref, taps_ref, table_ref, out_ref,
    x_buf, hist_buf, ext, spread, send_buf,
    load_sem, hist_send, hist_recv, own_sem, send_sem, recv_sem,
):
    blocks = x_buf.shape[0] // ROWS
    frames2 = x_buf.shape[1]
    frames = frames2 // 2
    keep = hist_buf.shape[1] // 2
    taps_count = taps_ref.shape[0]
    frame_len = taps_ref.shape[1]
    tm = lax.axis_index("tm")
    me = lax.axis_index("stn") * 2 + tm

    def load(b):
        rows = pl.ds(b * ROWS, ROWS)
        return pltpu.make_async_copy(x_ref.at[rows], x_buf.at[rows], load_sem.at[b])

    def history(b):
        rows = pl.ds(b * ROWS, ROWS)
        return pltpu.make_async_remote_copy(
            src_ref=x_ref.at[rows, pl.ds(frames2 - 2 * keep, 2 * keep)],
            dst_ref=hist_buf.at[rows],
            send_sem=hist_send.at[b],
            recv_sem=hist_recv.at[b],
            device_id={"tm": 1 - tm},
            device_id_type=MESH,
        )

    for b in range(blocks):
        load(b).start()

    barrier = pltpu.get_barrier_semaphore()
    for mask in range(1, group):
        other = flipped(me, mask, group)
        pl.semaphore_signal(
            barrier, inc=1, device_id={"stn": other // 2, "tm": other % 2}, device_id_type=MESH
        )
    pl.semaphore_wait(barrier, group - 1)

    for b in range(blocks):
        history(b).start()

    late = tm.astype(jnp.float32)

    def one_block(b, carry):
        load(b).wait()
        history(b).wait()

        def one_input(i, inner):
            row = b * ROWS + i
            h0 = hist_buf[row, pl.ds(0, keep, stride=2), :].astype(jnp.float32)
            h1 = hist_buf[row, pl.ds(1, keep, stride=2), :].astype(jnp.float32)
            ext[0, pl.ds(0, keep), :] = h0 * late
            ext[1, pl.ds(0, keep), :] = h1 * late + h0 * (1.0 - late)
            parts = []
            for g in range(2):
                ext[g, pl.ds(keep, frames), :] = x_buf[
                    row, pl.ds(g, frames, stride=2), :
                ].astype(jnp.float32)
                first = keep - (taps_count - 1)
                acc = taps_ref[0:1, :] * ext[g, pl.ds(first, frames), :]
                for j in range(1, taps_count):
                    acc = acc + taps_ref[j : j + 1, :] * ext[g, pl.ds(first + j, frames), :]
                parts.append(acc)
            filtered = jnp.concatenate(parts, axis=0)
            spectra = lax.dot_general(
                table_ref[...], filtered, (((1,), (1,)), ((), ())),
                precision=lax.Precision.HIGHEST, preferred_element_type=jnp.float32,
            )
            for g in range(2):
                spread[g, pl.ds(i, frame_len, stride=ROWS), :] = spectra[
                    :, g * frames : (g + 1) * frames
                ]
            return inner

        lax.fori_loop(0, ROWS, one_input, 0)
        share = frame_len * ROWS // group
        for g in range(2):
            send_buf[:, b, pl.ds(g * share, share), :] = (
                spread[g].reshape(group, share, frames).astype(jnp.bfloat16)
            )
        for mask in range(group - 1, 0, -1):
            other = flipped(me, mask, group)
            pltpu.make_async_remote_copy(
                src_ref=send_buf.at[other, b],
                dst_ref=out_ref.at[me, b],
                send_sem=send_sem.at[other],
                recv_sem=recv_sem.at[me],
                device_id={"stn": other // 2, "tm": other % 2},
                device_id_type=MESH,
            ).start()
        return carry

    lax.fori_loop(0, blocks, one_block, 0)
    own = pltpu.make_async_copy(send_buf.at[me], out_ref.at[me], own_sem)
    own.start()
    own.wait()
    for mask in range(1, group):
        other = flipped(me, mask, group)
        whole = pltpu.make_async_remote_copy(
            src_ref=send_buf.at[other],
            dst_ref=out_ref.at[other],
            send_sem=send_sem.at[other],
            recv_sem=recv_sem.at[other],
            device_id={"stn": other // 2, "tm": other % 2},
            device_id_type=MESH,
        )
        whole.wait_send()
        whole.wait_recv()


def correlate_kernel(scale, in_ref, out_ref):
    stations, halves, blocks, pair, frames = in_ref.shape
    inputs = stations * blocks * ROWS
    real = []
    imag = []
    for t in range(halves):
        both = in_ref[:, t].astype(jnp.float32).reshape(stations * blocks, pair, frames)
        real.append(both[:, :ROWS].reshape(inputs, frames))
        imag.append(both[:, ROWS:].reshape(inputs, frames))
    right = jnp.concatenate(real + imag, axis=1).astype(jnp.bfloat16)
    left = jnp.concatenate(imag + [-value for value in real], axis=1).astype(jnp.bfloat16)
    dims = (((1,), (1,)), ((), ()))
    out_ref[0] = scale * lax.dot_general(right, right, dims, preferred_element_type=jnp.float32)
    out_ref[1] = scale * lax.dot_general(left, right, dims, preferred_element_type=jnp.float32)


def kernel_shards(stations, halves, voltages, filter_taps):
    inputs_dev, sub_count, time_dev = voltages.shape
    taps_count, frame_len = filter_taps.shape
    frames = time_dev // frame_len
    group = stations * halves
    blocks = inputs_dev // ROWS
    keep = 16
    per_dev = frame_len // 2 // group
    table = jnp.asarray(np.ascontiguousarray(transform_table(frame_len, frame_len // 2).T))
    x = voltages.reshape(inputs_dev, sub_count, frames, frame_len)
    x = jnp.transpose(x, (0, 2, 1, 3)).reshape(inputs_dev, frames * sub_count, frame_len)
    rows = 2 * frame_len * ROWS // group
    vmem = pl.BlockSpec(memory_space=pltpu.VMEM)
    spectra = pl.pallas_call(
        functools.partial(spectra_kernel, group),
        out_shape=jax.ShapeDtypeStruct((group, blocks, rows, frames), jnp.bfloat16),
        in_specs=[pl.BlockSpec(memory_space=pl.ANY), vmem, vmem],
        out_specs=pl.BlockSpec(memory_space=pl.ANY),
        scratch_shapes=[
            pltpu.VMEM((inputs_dev, frames * 2, frame_len), jnp.int32),
            pltpu.VMEM((inputs_dev, keep * 2, frame_len), jnp.int32),
            pltpu.VMEM((2, keep + frames, frame_len), jnp.float32),
            pltpu.VMEM((2, frame_len * ROWS, frames), jnp.float32),
            pltpu.VMEM((group, blocks, rows, frames), jnp.bfloat16),
            pltpu.SemaphoreType.DMA((blocks,)),
            pltpu.SemaphoreType.DMA((blocks,)),
            pltpu.SemaphoreType.DMA((blocks,)),
            pltpu.SemaphoreType.DMA,
            pltpu.SemaphoreType.DMA((group,)),
            pltpu.SemaphoreType.DMA((group,)),
        ],
        compiler_params=pltpu.CompilerParams(
            collective_id=0, has_side_effects=True, vmem_limit_bytes=60 * 1024 * 1024
        ),
        name="spectra",
    )(x, filter_taps, table)
    spectra = spectra.reshape(stations, halves, blocks, sub_count * per_dev, 2 * ROWS, frames)
    inputs = stations * inputs_dev
    return pl.pallas_call(
        functools.partial(correlate_kernel, 1.0 / (frames * halves)),
        grid=(sub_count * per_dev,),
        out_shape=jax.ShapeDtypeStruct((2, sub_count, per_dev, inputs, inputs), jnp.float32),
        in_specs=[
            pl.BlockSpec(
                (stations, halves, blocks, None, 2 * ROWS, frames), lambda s: (0, 0, 0, s, 0, 0)
            )
        ],
        out_specs=pl.BlockSpec(
            (2, None, None, inputs, inputs), lambda s: (0, s // per_dev, s % per_dev, 0, 0)
        ),
        compiler_params=pltpu.CompilerParams(vmem_limit_bytes=50 * 1024 * 1024),
        name="correlate",
    )(spectra)


def shards(stations, halves, voltages, filter_taps):
    inputs_dev, sub_count, time_dev = voltages.shape
    taps_count, frame_len = filter_taps.shape
    group = stations * halves
    fits = (
        halves == 2
        and sub_count == 2
        and group & (group - 1) == 0
        and group <= 16
        and inputs_dev % ROWS == 0
        and frame_len == 128
        and time_dev == 128 * frame_len
        and taps_count == 16
    )
    if fits:
        return kernel_shards(stations, halves, voltages, filter_taps)
    return general_shards(voltages, filter_taps)


def solution(mesh):
    placed = (P("stn", "band", "tm"), P())
    return jax.shard_map(
        functools.partial(shards, mesh.shape["stn"], mesh.shape["tm"]),
        mesh=mesh,
        in_specs=placed,
        out_specs=P(None, None, ("band", "stn", "tm"), None, None),
        check_vma=False,
    )
```

```python
import functools
import math

import jax
import jax.numpy as jnp
import numpy as np
from jax import lax
from jax.experimental import pallas as pl
from jax.experimental.pallas import tpu as pltpu
from jax.sharding import PartitionSpec as P

MESH = pl.DeviceIdType.MESH
ROWS = 8
DEFERRED = 5


def passed_along(value, axis, steps):
    count = lax.axis_size(axis)
    pairs = [(source, (source + steps) % count) for source in range(count)]
    return lax.ppermute(value, axis, pairs)


def transform_table(frame_len, chan_count):
    sample_index = np.arange(frame_len)[:, None]
    chan_index = np.arange(chan_count)[None, :]
    phase = (2 * chan_index + 1) * sample_index % (2 * frame_len)
    angle = phase.astype(np.float64) * (math.pi / frame_len)
    factor = 1.0 / math.sqrt(frame_len)
    cosine = np.cos(angle) * factor
    sine = -np.sin(angle) * factor
    table = np.stack([cosine, sine], axis=2).reshape(frame_len, 2 * chan_count)
    return table.astype(np.float32)


def arrange(blocks):
    stations, blocks_time, per_dev, parts_two, inputs_dev, sub_count, spec_dev = blocks.shape
    ordered = jnp.transpose(blocks, (3, 5, 2, 0, 4, 1, 6))
    return ordered.reshape(
        parts_two, sub_count, per_dev, stations * inputs_dev, blocks_time * spec_dev
    )


def correlate(stacked):
    real_in = stacked[0]
    imag_in = stacked[1]
    right_side = jnp.concatenate([real_in, imag_in], axis=-1)
    left_imag = jnp.concatenate([imag_in, -real_in], axis=-1)
    real_part = jnp.einsum(
        "gcis,gcjs->gcij", right_side, right_side, preferred_element_type=jnp.float32
    )
    imag_part = jnp.einsum(
        "gcis,gcjs->gcij", left_imag, right_side, preferred_element_type=jnp.float32
    )
    return jnp.stack([real_part, imag_part])


def general_shards(voltages, filter_taps):
    inputs_dev, sub_count, time_dev = voltages.shape
    taps_count, frame_len = filter_taps.shape
    spec_dev = time_dev // frame_len
    chan_count = frame_len // 2
    lagging = taps_count - 1
    frames = voltages.astype(jnp.bfloat16).reshape(inputs_dev, sub_count, spec_dev, frame_len)
    last_frames = frames[:, :, spec_dev - lagging :, :]
    received = passed_along(last_frames, "tm", 1)
    earlier = jnp.concatenate([jnp.zeros_like(received[:, :1]), received[:, :-1]], axis=1)
    history = jnp.where(lax.axis_index("tm") == 0, earlier, received)
    extended = jnp.concatenate([history, frames], axis=2).astype(jnp.float32)
    filtered = filter_taps[0] * extended[:, :, 0:spec_dev]
    for tap_index in range(1, taps_count):
        filtered = (
            filtered + filter_taps[tap_index] * extended[:, :, tap_index : tap_index + spec_dev]
        )
    table = jnp.asarray(transform_table(frame_len, chan_count))
    spectra = lax.dot_general(
        table,
        filtered.reshape(-1, frame_len),
        (((0,), (1,)), ((), ())),
        precision=lax.Precision.HIGHEST,
        preferred_element_type=jnp.float32,
    ).astype(jnp.bfloat16)
    stations = lax.axis_size("stn")
    halves = lax.axis_size("tm")
    scale = 1.0 / (spec_dev * halves)
    moved = lax.all_to_all(spectra[None], ("stn", "tm"), split_axis=1, concat_axis=0, tiled=True)
    per_dev = moved.shape[1] // 2
    blocks = moved.reshape(stations, halves, per_dev, 2, inputs_dev, sub_count, spec_dev)
    result = correlate(arrange(blocks))
    return result * scale


def flipped(index, mask, count):
    total = 0
    bit = 1
    while bit < count:
        value = (index // bit) % 2
        total = total + (1 - value if mask & bit else value) * bit
        bit *= 2
    return total


def spectra_kernel(
    group, x_ref, taps_in, table_in, *refs
):
    half = group // 2
    out_ref, far_refs, scratch = refs[0], refs[1 : 1 + DEFERRED], refs[1 + DEFERRED :]
    taps_ref, table_ref, x_buf, hist_buf, ext, spread, send_buf = scratch[:7]
    small_sem, load_sem, hist_send, hist_recv, own_sem, far_sem, send_sem, recv_sem = scratch[7:]
    early = send_buf.shape[2] - 2 * ROWS
    blocks = x_buf.shape[0] // ROWS
    frames2 = x_buf.shape[1]
    frames = frames2 // 2
    keep = hist_buf.shape[1] // 2
    taps_count = taps_ref.shape[0]
    frame_len = taps_ref.shape[1]
    tm = lax.axis_index("tm")
    me = lax.axis_index("stn") * 2 + tm

    def load(b):
        rows = pl.ds(b * ROWS, ROWS)
        return pltpu.make_async_copy(x_ref.at[rows], x_buf.at[rows], load_sem.at[b])

    def history(b):
        rows = pl.ds(b * ROWS, ROWS)
        return pltpu.make_async_remote_copy(
            src_ref=x_ref.at[rows, pl.ds(frames2 - 2 * keep, 2 * keep)],
            dst_ref=hist_buf.at[rows],
            send_sem=hist_send.at[b],
            recv_sem=hist_recv.at[b],
            device_id={"tm": 1 - tm},
            device_id_type=MESH,
        )

    small = [
        pltpu.make_async_copy(taps_in, taps_ref, small_sem.at[0]),
        pltpu.make_async_copy(table_in, table_ref, small_sem.at[1]),
    ]
    for copy in small:
        copy.start()
    for b in range(blocks):
        load(b).start()

    barrier = pltpu.get_barrier_semaphore()
    for mask in range(1, group):
        other = flipped(me, mask, group)
        pl.semaphore_signal(
            barrier, inc=1, device_id={"stn": other // 2, "tm": other % 2}, device_id_type=MESH
        )
    pl.semaphore_wait(barrier, group - 1)

    for b in range(blocks):
        history(b).start()

    for copy in small:
        copy.wait()
    late = tm.astype(jnp.float32)

    def one_block(b, carry):
        load(b).wait()
        history(b).wait()

        def one_input(i, inner):
            row = b * ROWS + i
            h0 = hist_buf[row, pl.ds(0, keep, stride=2), :].astype(jnp.float32)
            h1 = hist_buf[row, pl.ds(1, keep, stride=2), :].astype(jnp.float32)
            ext[0, pl.ds(0, keep), :] = h0 * late
            ext[1, pl.ds(0, keep), :] = h1 * late + h0 * (1.0 - late)
            parts = []
            for g in range(2):
                ext[g, pl.ds(keep, frames), :] = x_buf[
                    row, pl.ds(g, frames, stride=2), :
                ].astype(jnp.float32)
                first = keep - (taps_count - 1)
                acc = taps_ref[0:1, :] * ext[g, pl.ds(first, frames), :]
                for j in range(1, taps_count):
                    acc = acc + taps_ref[j : j + 1, :] * ext[g, pl.ds(first + j, frames), :]
                parts.append(acc)
            filtered = jnp.concatenate(parts, axis=0)
            spectra = lax.dot_general(
                table_ref[...], filtered, (((1,), (1,)), ((), ())),
                precision=lax.Precision.HIGHEST, preferred_element_type=jnp.float32,
            )
            for g in range(2):
                spread[g, pl.ds(i, frame_len, stride=ROWS), :] = spectra[
                    :, g * frames : (g + 1) * frames
                ]
            return inner

        lax.fori_loop(0, ROWS, one_input, 0)
        share = frame_len * ROWS // group
        for g in range(2):
            send_buf[:, b, pl.ds(g * share, share), :] = (
                spread[g].reshape(group, share, frames).astype(jnp.bfloat16)
            )
        for mask in range(group - 1, 0, -1):
            other = flipped(me, mask, group)
            rows = pl.ds(0, early if half <= mask < half + DEFERRED else early + 2 * ROWS)
            pltpu.make_async_remote_copy(
                src_ref=send_buf.at[other, b, rows],
                dst_ref=out_ref.at[me, b, rows],
                send_sem=send_sem.at[other],
                recv_sem=recv_sem.at[me],
                device_id={"stn": other // 2, "tm": other % 2},
                device_id_type=MESH,
            ).start()
        return carry

    lax.fori_loop(0, blocks, one_block, 0)
    own = pltpu.make_async_copy(send_buf.at[me], out_ref.at[me], own_sem)
    own.start()
    kept = []
    for m in range(DEFERRED):
        other = flipped(me, half + m, group)
        kept.append(
            pltpu.make_async_copy(
                send_buf.at[other, :, pl.ds(early, 2 * ROWS)], far_refs[m], far_sem.at[m]
            )
        )
        kept[m].start()
    own.wait()
    for copy in kept:
        copy.wait()
    for mask in range(1, group):
        other = flipped(me, mask, group)
        rows = pl.ds(0, early if half <= mask < half + DEFERRED else early + 2 * ROWS)
        whole = pltpu.make_async_remote_copy(
            src_ref=send_buf.at[other, :, rows],
            dst_ref=out_ref.at[other, :, rows],
            send_sem=send_sem.at[other],
            recv_sem=recv_sem.at[other],
            device_id={"stn": other // 2, "tm": other % 2},
            device_id_type=MESH,
        )
        whole.wait_send()
        whole.wait_recv()


def products(scale, halves_in, out_ref):
    real = []
    imag = []
    for value in halves_in:
        stations, blocks, pair, frames = value.shape
        inputs = stations * blocks * ROWS
        both = value.astype(jnp.float32).reshape(stations * blocks, pair, frames)
        real.append(both[:, :ROWS].reshape(inputs, frames))
        imag.append(both[:, ROWS:].reshape(inputs, frames))
    right = jnp.concatenate(real + imag, axis=1).astype(jnp.bfloat16)
    left = jnp.concatenate(imag + [-value for value in real], axis=1).astype(jnp.bfloat16)
    dims = (((1,), (1,)), ((), ()))
    left = jnp.concatenate([right * scale, left * scale], axis=0)
    product = lax.dot_general(left, right, dims, preferred_element_type=jnp.float32)
    out_ref[...] = product.reshape(2, inputs, inputs)


def correlate_kernel(scale, in_ref, out_ref):
    step = pl.program_id(0)
    halves = in_ref.shape[1]
    products(scale, [in_ref[:, t, :, step] for t in range(halves)], out_ref)


def last_kernel(scale, in_ref, *refs):
    half = in_ref.shape[0] * in_ref.shape[1] // 2
    far_refs, out_ref, full = refs[:DEFERRED], refs[DEFERRED + 1], refs[DEFERRED + 2]
    halves = in_ref.shape[1]
    step = in_ref.shape[3] - 1
    me = lax.axis_index("stn") * halves + lax.axis_index("tm")
    full[...] = in_ref[:, :, :, step]
    for m in range(DEFERRED):
        other = flipped(me, half + m, 2 * half)
        full[other // halves, other % halves] = far_refs[m][...]
    products(scale, [full[:, t] for t in range(halves)], out_ref)


def kernel_shards(stations, halves, voltages, filter_taps):
    inputs_dev, sub_count, time_dev = voltages.shape
    taps_count, frame_len = filter_taps.shape
    frames = time_dev // frame_len
    group = stations * halves
    blocks = inputs_dev // ROWS
    keep = 16
    per_dev = frame_len // 2 // group
    table = jnp.asarray(np.ascontiguousarray(transform_table(frame_len, frame_len // 2).T))
    x = voltages.reshape(inputs_dev, sub_count, frames, frame_len)
    x = jnp.transpose(x, (0, 2, 1, 3)).reshape(inputs_dev, frames * sub_count, frame_len)
    rows = 2 * frame_len * ROWS // group
    vmem = pl.BlockSpec(memory_space=pltpu.VMEM)
    anywhere = pl.BlockSpec(memory_space=pl.ANY)
    half = group // 2
    far_shape = jax.ShapeDtypeStruct((blocks, 2 * ROWS, frames), jnp.bfloat16)
    spectra, *far = pl.pallas_call(
        functools.partial(spectra_kernel, group),
        out_shape=[jax.ShapeDtypeStruct((group, blocks, rows, frames), jnp.bfloat16)]
        + [far_shape] * DEFERRED,
        in_specs=[anywhere] + [pl.BlockSpec(memory_space=pltpu.HBM)] * 2,
        out_specs=[vmem] * (1 + DEFERRED),
        scratch_shapes=[
            pltpu.VMEM((taps_count, frame_len), jnp.float32),
            pltpu.VMEM((frame_len, frame_len), jnp.float32),
            pltpu.VMEM((inputs_dev, frames * 2, frame_len), jnp.int32),
            pltpu.VMEM((inputs_dev, keep * 2, frame_len), jnp.int32),
            pltpu.VMEM((2, keep + frames, frame_len), jnp.float32),
            pltpu.VMEM((2, frame_len * ROWS, frames), jnp.float32),
            pltpu.VMEM((group, blocks, rows, frames), jnp.bfloat16),
            pltpu.SemaphoreType.DMA((2,)),
            pltpu.SemaphoreType.DMA((blocks,)),
            pltpu.SemaphoreType.DMA((blocks,)),
            pltpu.SemaphoreType.DMA((blocks,)),
            pltpu.SemaphoreType.DMA,
            pltpu.SemaphoreType.DMA((DEFERRED,)),
            pltpu.SemaphoreType.DMA((group,)),
            pltpu.SemaphoreType.DMA((group,)),
        ],
        compiler_params=pltpu.CompilerParams(
            collective_id=0, has_side_effects=True, vmem_limit_bytes=40 * 1024 * 1024
        ),
        name="spectra",
    )(x, filter_taps, table)
    spectra = spectra.reshape(stations, halves, blocks, sub_count * per_dev, 2 * ROWS, frames)
    received = [
        lax.ppermute(
            far[m], ("stn", "tm"), [(source, source ^ (half + m)) for source in range(group)]
        )
        for m in range(DEFERRED)
    ]
    inputs = stations * inputs_dev
    scale = 1.0 / (frames * halves)
    steps = sub_count * per_dev
    out_shape = jax.ShapeDtypeStruct((2, sub_count, per_dev, inputs, inputs), jnp.float32)
    flops = 8 * inputs * inputs * halves * frames
    partly = pl.pallas_call(
        functools.partial(correlate_kernel, scale),
        grid=(steps - 1,),
        out_shape=out_shape,
        in_specs=[vmem],
        out_specs=pl.BlockSpec(
            (2, None, None, inputs, inputs), lambda s: (0, s // per_dev, s % per_dev, 0, 0)
        ),
        compiler_params=pltpu.CompilerParams(vmem_limit_bytes=40 * 1024 * 1024),
        cost_estimate=pl.CostEstimate(
            flops=(steps - 1) * flops,
            bytes_accessed=(steps - 1) * 8 * inputs * inputs,
            transcendentals=0,
        ),
        name="correlate",
    )(spectra)
    return pl.pallas_call(
        functools.partial(last_kernel, scale),
        grid=(1,),
        out_shape=out_shape,
        in_specs=[vmem] * (1 + DEFERRED) + [anywhere],
        out_specs=pl.BlockSpec(
            (2, None, None, inputs, inputs), lambda s: (0, sub_count - 1, per_dev - 1, 0, 0)
        ),
        scratch_shapes=[pltpu.VMEM((stations, halves, blocks, 2 * ROWS, frames), jnp.bfloat16)],
        input_output_aliases={1 + DEFERRED: 0},
        compiler_params=pltpu.CompilerParams(vmem_limit_bytes=40 * 1024 * 1024),
        cost_estimate=pl.CostEstimate(
            flops=flops, bytes_accessed=8 * inputs * inputs, transcendentals=0
        ),
        name="last",
    )(spectra, *received, partly)


def shards(stations, halves, voltages, filter_taps):
    inputs_dev, sub_count, time_dev = voltages.shape
    taps_count, frame_len = filter_taps.shape
    group = stations * halves
    fits = (
        halves == 2
        and sub_count == 2
        and group & (group - 1) == 0
        and group == 16
        and inputs_dev % ROWS == 0
        and frame_len == 128
        and time_dev == 128 * frame_len
        and taps_count == 16
    )
    if fits:
        return kernel_shards(stations, halves, voltages, filter_taps)
    return general_shards(voltages, filter_taps)


def solution(mesh):
    placed = (P("stn", "band", "tm"), P())
    return jax.shard_map(
        functools.partial(shards, mesh.shape["stn"], mesh.shape["tm"]),
        mesh=mesh,
        in_specs=placed,
        out_specs=P(None, None, ("band", "stn", "tm"), None, None),
        check_vma=False,
    )
```

```python
import functools
import math

import jax
import jax.numpy as jnp
import numpy as np
from jax import lax
from jax.experimental import pallas as pl
from jax.experimental.pallas import tpu as pltpu
from jax.sharding import PartitionSpec as P

MESH = pl.DeviceIdType.MESH
ROWS = 8


def passed_along(value, axis, steps):
    count = lax.axis_size(axis)
    pairs = [(source, (source + steps) % count) for source in range(count)]
    return lax.ppermute(value, axis, pairs)


def transform_table(frame_len, chan_count):
    sample_index = np.arange(frame_len)[:, None]
    chan_index = np.arange(chan_count)[None, :]
    phase = (2 * chan_index + 1) * sample_index % (2 * frame_len)
    angle = phase.astype(np.float64) * (math.pi / frame_len)
    factor = 1.0 / math.sqrt(frame_len)
    cosine = np.cos(angle) * factor
    sine = -np.sin(angle) * factor
    table = np.stack([cosine, sine], axis=2).reshape(frame_len, 2 * chan_count)
    return table.astype(np.float32)


def arrange(blocks):
    stations, blocks_time, per_dev, parts_two, inputs_dev, sub_count, spec_dev = blocks.shape
    ordered = jnp.transpose(blocks, (3, 5, 2, 0, 4, 1, 6))
    return ordered.reshape(
        parts_two, sub_count, per_dev, stations * inputs_dev, blocks_time * spec_dev
    )


def correlate(stacked):
    real_in = stacked[0]
    imag_in = stacked[1]
    right_side = jnp.concatenate([real_in, imag_in], axis=-1)
    left_imag = jnp.concatenate([imag_in, -real_in], axis=-1)
    real_part = jnp.einsum(
        "gcis,gcjs->gcij", right_side, right_side, preferred_element_type=jnp.float32
    )
    imag_part = jnp.einsum(
        "gcis,gcjs->gcij", left_imag, right_side, preferred_element_type=jnp.float32
    )
    return jnp.stack([real_part, imag_part])


def general_shards(voltages, filter_taps):
    inputs_dev, sub_count, time_dev = voltages.shape
    taps_count, frame_len = filter_taps.shape
    spec_dev = time_dev // frame_len
    chan_count = frame_len // 2
    lagging = taps_count - 1
    frames = voltages.astype(jnp.bfloat16).reshape(inputs_dev, sub_count, spec_dev, frame_len)
    last_frames = frames[:, :, spec_dev - lagging :, :]
    received = passed_along(last_frames, "tm", 1)
    earlier = jnp.concatenate([jnp.zeros_like(received[:, :1]), received[:, :-1]], axis=1)
    history = jnp.where(lax.axis_index("tm") == 0, earlier, received)
    extended = jnp.concatenate([history, frames], axis=2).astype(jnp.float32)
    filtered = filter_taps[0] * extended[:, :, 0:spec_dev]
    for tap_index in range(1, taps_count):
        filtered = (
            filtered + filter_taps[tap_index] * extended[:, :, tap_index : tap_index + spec_dev]
        )
    table = jnp.asarray(transform_table(frame_len, chan_count))
    spectra = lax.dot_general(
        table,
        filtered.reshape(-1, frame_len),
        (((0,), (1,)), ((), ())),
        precision=lax.Precision.HIGHEST,
        preferred_element_type=jnp.float32,
    ).astype(jnp.bfloat16)
    stations = lax.axis_size("stn")
    halves = lax.axis_size("tm")
    scale = 1.0 / (spec_dev * halves)
    moved = lax.all_to_all(spectra[None], ("stn", "tm"), split_axis=1, concat_axis=0, tiled=True)
    per_dev = moved.shape[1] // 2
    blocks = moved.reshape(stations, halves, per_dev, 2, inputs_dev, sub_count, spec_dev)
    result = correlate(arrange(blocks))
    return result * scale


def flipped(index, mask, count):
    total = 0
    bit = 1
    while bit < count:
        value = (index // bit) % 2
        total = total + (1 - value if mask & bit else value) * bit
        bit *= 2
    return total


def spectra_kernel(
    group, x_ref, taps_ref, table_ref, out_ref,
    x_buf, hist_buf, ext, spread, send_buf,
    load_sem, hist_send, hist_recv, own_sem, send_sem, recv_sem,
):
    blocks = x_buf.shape[0] // ROWS
    frames2 = x_buf.shape[1]
    frames = frames2 // 2
    keep = hist_buf.shape[1] // 2
    taps_count = taps_ref.shape[0]
    frame_len = taps_ref.shape[1]
    tm = lax.axis_index("tm")
    me = lax.axis_index("stn") * 2 + tm

    def load(b):
        rows = pl.ds(b * ROWS, ROWS)
        return pltpu.make_async_copy(x_ref.at[rows], x_buf.at[rows], load_sem.at[b])

    def history(b):
        rows = pl.ds(b * ROWS, ROWS)
        return pltpu.make_async_remote_copy(
            src_ref=x_ref.at[rows, pl.ds(frames2 - 2 * keep, 2 * keep)],
            dst_ref=hist_buf.at[rows],
            send_sem=hist_send.at[b],
            recv_sem=hist_recv.at[b],
            device_id={"tm": 1 - tm},
            device_id_type=MESH,
        )

    for b in range(blocks):
        load(b).start()

    barrier = pltpu.get_barrier_semaphore()
    for mask in range(1, group):
        other = flipped(me, mask, group)
        pl.semaphore_signal(
            barrier, inc=1, device_id={"stn": other // 2, "tm": other % 2}, device_id_type=MESH
        )
    pl.semaphore_wait(barrier, group - 1)

    for b in range(blocks):
        history(b).start()

    late = tm.astype(jnp.float32)

    def one_block(b, carry):
        load(b).wait()
        history(b).wait()

        def one_input(i, inner):
            row = b * ROWS + i
            h0 = hist_buf[row, pl.ds(0, keep, stride=2), :].astype(jnp.float32)
            h1 = hist_buf[row, pl.ds(1, keep, stride=2), :].astype(jnp.float32)
            ext[0, pl.ds(0, keep), :] = h0 * late
            ext[1, pl.ds(0, keep), :] = h1 * late + h0 * (1.0 - late)
            parts = []
            for g in range(2):
                ext[g, pl.ds(keep, frames), :] = x_buf[
                    row, pl.ds(g, frames, stride=2), :
                ].astype(jnp.float32)
                first = keep - (taps_count - 1)
                acc = taps_ref[0:1, :] * ext[g, pl.ds(first, frames), :]
                for j in range(1, taps_count):
                    acc = acc + taps_ref[j : j + 1, :] * ext[g, pl.ds(first + j, frames), :]
                parts.append(acc)
            filtered = jnp.concatenate(parts, axis=0)
            spectra = lax.dot_general(
                table_ref[...], filtered, (((1,), (1,)), ((), ())),
                precision=lax.Precision.HIGHEST, preferred_element_type=jnp.float32,
            )
            for g in range(2):
                spread[g, pl.ds(i, frame_len, stride=ROWS), :] = spectra[
                    :, g * frames : (g + 1) * frames
                ]
            return inner

        lax.fori_loop(0, ROWS, one_input, 0, unroll=4)
        share = frame_len * ROWS // group
        for g in range(2):
            send_buf[:, b, pl.ds(g * share, share), :] = (
                spread[g].reshape(group, share, frames).astype(jnp.bfloat16)
            )
        for mask in range(group - 1, 0, -1):
            other = flipped(me, mask, group)
            pltpu.make_async_remote_copy(
                src_ref=send_buf.at[other, b],
                dst_ref=out_ref.at[me, b],
                send_sem=send_sem.at[other],
                recv_sem=recv_sem.at[me],
                device_id={"stn": other // 2, "tm": other % 2},
                device_id_type=MESH,
            ).start()
        return carry

    lax.fori_loop(0, blocks, one_block, 0)
    own = pltpu.make_async_copy(send_buf.at[me], out_ref.at[me], own_sem)
    own.start()
    own.wait()
    for mask in range(1, group):
        other = flipped(me, mask, group)
        whole = pltpu.make_async_remote_copy(
            src_ref=send_buf.at[other],
            dst_ref=out_ref.at[other],
            send_sem=send_sem.at[other],
            recv_sem=recv_sem.at[other],
            device_id={"stn": other // 2, "tm": other % 2},
            device_id_type=MESH,
        )
        whole.wait_send()
        whole.wait_recv()


def correlate_kernel(in_ref, out_ref):
    stations, halves, blocks, _, pair, frames = in_ref.shape
    inputs = stations * blocks * ROWS
    step = pl.program_id(0)
    real = []
    imag = []
    for t in range(halves):
        both = in_ref[:, t, :, step].astype(jnp.float32)
        both = both.reshape(stations * blocks, pair, frames)
        real.append(both[:, :ROWS].reshape(inputs, frames))
        imag.append(both[:, ROWS:].reshape(inputs, frames))
    right = jnp.concatenate(real + imag, axis=1).astype(jnp.bfloat16)
    left = jnp.concatenate(imag + [-value for value in real], axis=1).astype(jnp.bfloat16)
    dims = (((1,), (1,)), ((), ()))
    left = jnp.concatenate([right, left], axis=0)
    product = lax.dot_general(left, right, dims, preferred_element_type=jnp.float32)
    out_ref[...] = product.reshape(2, inputs, inputs)


def kernel_shards(stations, halves, voltages, filter_taps):
    inputs_dev, sub_count, time_dev = voltages.shape
    taps_count, frame_len = filter_taps.shape
    frames = time_dev // frame_len
    group = stations * halves
    blocks = inputs_dev // ROWS
    keep = 16
    per_dev = frame_len // 2 // group
    share = np.float32(1.0 / math.sqrt(frames * halves))
    table = jnp.asarray(np.ascontiguousarray(transform_table(frame_len, frame_len // 2).T) * share)
    x = voltages.reshape(inputs_dev, sub_count, frames, frame_len)
    x = jnp.transpose(x, (0, 2, 1, 3)).reshape(inputs_dev, frames * sub_count, frame_len)
    rows = 2 * frame_len * ROWS // group
    vmem = pl.BlockSpec(memory_space=pltpu.VMEM)
    spectra = pl.pallas_call(
        functools.partial(spectra_kernel, group),
        out_shape=jax.ShapeDtypeStruct((group, blocks, rows, frames), jnp.bfloat16),
        in_specs=[pl.BlockSpec(memory_space=pl.ANY), vmem, vmem],
        out_specs=vmem,
        scratch_shapes=[
            pltpu.VMEM((inputs_dev, frames * 2, frame_len), jnp.int32),
            pltpu.VMEM((inputs_dev, keep * 2, frame_len), jnp.int32),
            pltpu.VMEM((2, keep + frames, frame_len), jnp.float32),
            pltpu.VMEM((2, frame_len * ROWS, frames), jnp.float32),
            pltpu.VMEM((group, blocks, rows, frames), jnp.bfloat16),
            pltpu.SemaphoreType.DMA((blocks,)),
            pltpu.SemaphoreType.DMA((blocks,)),
            pltpu.SemaphoreType.DMA((blocks,)),
            pltpu.SemaphoreType.DMA,
            pltpu.SemaphoreType.DMA((group,)),
            pltpu.SemaphoreType.DMA((group,)),
        ],
        compiler_params=pltpu.CompilerParams(
            collective_id=0, has_side_effects=True, vmem_limit_bytes=40960 * 1024
        ),
        name="spectra",
    )(x, filter_taps, table)
    spectra = spectra.reshape(stations, halves, blocks, sub_count * per_dev, 2 * ROWS, frames)
    inputs = stations * inputs_dev
    return pl.pallas_call(
        correlate_kernel,
        grid=(sub_count * per_dev,),
        out_shape=jax.ShapeDtypeStruct((2, sub_count, per_dev, inputs, inputs), jnp.float32),
        in_specs=[vmem],
        out_specs=pl.BlockSpec(
            (2, None, None, inputs, inputs), lambda s: (0, s // per_dev, s % per_dev, 0, 0)
        ),
        compiler_params=pltpu.CompilerParams(vmem_limit_bytes=40 * 1024 * 1024),
        name="correlate",
    )(spectra)


def shards(stations, halves, voltages, filter_taps):
    inputs_dev, sub_count, time_dev = voltages.shape
    taps_count, frame_len = filter_taps.shape
    group = stations * halves
    fits = (
        halves == 2
        and sub_count == 2
        and group & (group - 1) == 0
        and group <= 16
        and inputs_dev % ROWS == 0
        and frame_len == 128
        and time_dev == 128 * frame_len
        and taps_count == 16
    )
    if fits:
        return kernel_shards(stations, halves, voltages, filter_taps)
    return general_shards(voltages, filter_taps)


def solution(mesh):
    placed = (P("stn", "band", "tm"), P())
    return jax.shard_map(
        functools.partial(shards, mesh.shape["stn"], mesh.shape["tm"]),
        mesh=mesh,
        in_specs=placed,
        out_specs=P(None, None, ("band", "stn", "tm"), None, None),
        check_vma=False,
    )
```

```python
import functools
import math

import jax
import jax.numpy as jnp
import numpy as np
from jax import lax
from jax.experimental import pallas as pl
from jax.experimental.pallas import tpu as pltpu
from jax.sharding import PartitionSpec as P

MESH = pl.DeviceIdType.MESH
ROWS = 8


def passed_along(value, axis, steps):
    count = lax.axis_size(axis)
    pairs = [(source, (source + steps) % count) for source in range(count)]
    return lax.ppermute(value, axis, pairs)


def transform_table(frame_len, chan_count):
    sample_index = np.arange(frame_len)[:, None]
    chan_index = np.arange(chan_count)[None, :]
    phase = (2 * chan_index + 1) * sample_index % (2 * frame_len)
    angle = phase.astype(np.float64) * (math.pi / frame_len)
    factor = 1.0 / math.sqrt(frame_len)
    cosine = np.cos(angle) * factor
    sine = -np.sin(angle) * factor
    table = np.stack([cosine, sine], axis=2).reshape(frame_len, 2 * chan_count)
    return table.astype(np.float32)


def arrange(blocks):
    stations, blocks_time, per_dev, parts_two, inputs_dev, sub_count, spec_dev = blocks.shape
    ordered = jnp.transpose(blocks, (3, 5, 2, 0, 4, 1, 6))
    return ordered.reshape(
        parts_two, sub_count, per_dev, stations * inputs_dev, blocks_time * spec_dev
    )


def correlate(stacked):
    real_in = stacked[0]
    imag_in = stacked[1]
    right_side = jnp.concatenate([real_in, imag_in], axis=-1)
    left_imag = jnp.concatenate([imag_in, -real_in], axis=-1)
    real_part = jnp.einsum(
        "gcis,gcjs->gcij", right_side, right_side, preferred_element_type=jnp.float32
    )
    imag_part = jnp.einsum(
        "gcis,gcjs->gcij", left_imag, right_side, preferred_element_type=jnp.float32
    )
    return jnp.stack([real_part, imag_part])


def general_shards(voltages, filter_taps):
    inputs_dev, sub_count, time_dev = voltages.shape
    taps_count, frame_len = filter_taps.shape
    spec_dev = time_dev // frame_len
    chan_count = frame_len // 2
    lagging = taps_count - 1
    frames = voltages.astype(jnp.bfloat16).reshape(inputs_dev, sub_count, spec_dev, frame_len)
    last_frames = frames[:, :, spec_dev - lagging :, :]
    received = passed_along(last_frames, "tm", 1)
    earlier = jnp.concatenate([jnp.zeros_like(received[:, :1]), received[:, :-1]], axis=1)
    history = jnp.where(lax.axis_index("tm") == 0, earlier, received)
    extended = jnp.concatenate([history, frames], axis=2).astype(jnp.float32)
    filtered = filter_taps[0] * extended[:, :, 0:spec_dev]
    for tap_index in range(1, taps_count):
        filtered = (
            filtered + filter_taps[tap_index] * extended[:, :, tap_index : tap_index + spec_dev]
        )
    table = jnp.asarray(transform_table(frame_len, chan_count))
    spectra = lax.dot_general(
        table,
        filtered.reshape(-1, frame_len),
        (((0,), (1,)), ((), ())),
        precision=lax.Precision.HIGHEST,
        preferred_element_type=jnp.float32,
    ).astype(jnp.bfloat16)
    stations = lax.axis_size("stn")
    halves = lax.axis_size("tm")
    scale = 1.0 / (spec_dev * halves)
    moved = lax.all_to_all(spectra[None], ("stn", "tm"), split_axis=1, concat_axis=0, tiled=True)
    per_dev = moved.shape[1] // 2
    blocks = moved.reshape(stations, halves, per_dev, 2, inputs_dev, sub_count, spec_dev)
    result = correlate(arrange(blocks))
    return result * scale


def flipped(index, mask, count):
    total = 0
    bit = 1
    while bit < count:
        value = (index // bit) % 2
        total = total + (1 - value if mask & bit else value) * bit
        bit *= 2
    return total


def spectra_kernel(
    group, x_ref, taps_ref, table_ref, out_ref,
    x_buf, hist_buf, ext, spread, send_buf,
    load_sem, hist_send, hist_recv, own_sem, send_sem, recv_sem,
):
    blocks = x_buf.shape[0] // ROWS
    frames2 = x_buf.shape[1]
    frames = frames2 // 2
    keep = hist_buf.shape[1] // 2
    taps_count = taps_ref.shape[0]
    frame_len = taps_ref.shape[1]
    tm = lax.axis_index("tm")
    me = lax.axis_index("stn") * 2 + tm

    def load(b):
        rows = pl.ds(b * ROWS, ROWS)
        return pltpu.make_async_copy(x_ref.at[rows], x_buf.at[rows], load_sem.at[b])

    def history(b):
        rows = pl.ds(b * ROWS, ROWS)
        return pltpu.make_async_remote_copy(
            src_ref=x_ref.at[rows, pl.ds(frames2 - 2 * keep, 2 * keep)],
            dst_ref=hist_buf.at[rows],
            send_sem=hist_send.at[b],
            recv_sem=hist_recv.at[b],
            device_id={"tm": 1 - tm},
            device_id_type=MESH,
        )

    for b in range(blocks):
        load(b).start()

    barrier = pltpu.get_barrier_semaphore()
    for mask in range(1, group):
        other = flipped(me, mask, group)
        pl.semaphore_signal(
            barrier, inc=1, device_id={"stn": other // 2, "tm": other % 2}, device_id_type=MESH
        )
    pl.semaphore_wait(barrier, group - 1)

    for b in range(blocks):
        history(b).start()

    late = tm.astype(jnp.float32)

    def one_block(b, carry):
        load(b).wait()
        history(b).wait()

        def one_input(i, inner):
            row = b * ROWS + i
            h0 = hist_buf[row, pl.ds(0, keep, stride=2), :].astype(jnp.float32)
            h1 = hist_buf[row, pl.ds(1, keep, stride=2), :].astype(jnp.float32)
            ext[0, pl.ds(0, keep), :] = h0 * late
            ext[1, pl.ds(0, keep), :] = h1 * late + h0 * (1.0 - late)
            parts = []
            for g in range(2):
                ext[g, pl.ds(keep, frames), :] = x_buf[
                    row, pl.ds(g, frames, stride=2), :
                ].astype(jnp.float32)
                first = keep - (taps_count - 1)
                acc = taps_ref[0:1, :] * ext[g, pl.ds(first, frames), :]
                for j in range(1, taps_count):
                    acc = acc + taps_ref[j : j + 1, :] * ext[g, pl.ds(first + j, frames), :]
                parts.append(acc)
            filtered = jnp.concatenate(parts, axis=0)
            spectra = lax.dot_general(
                table_ref[...], filtered, (((1,), (1,)), ((), ())),
                precision=lax.Precision.HIGHEST, preferred_element_type=jnp.float32,
            )
            for g in range(2):
                spread[g, pl.ds(i, frame_len, stride=ROWS), :] = spectra[
                    :, g * frames : (g + 1) * frames
                ]
            return inner

        lax.fori_loop(0, ROWS, one_input, 0, unroll=8)
        share = frame_len * ROWS // group
        for g in range(2):
            send_buf[:, b, pl.ds(g * share, share), :] = (
                spread[g].reshape(group, share, frames).astype(jnp.bfloat16)
            )
        for mask in range(group - 1, 0, -1):
            other = flipped(me, mask, group)
            pltpu.make_async_remote_copy(
                src_ref=send_buf.at[other, b],
                dst_ref=out_ref.at[me, b],
                send_sem=send_sem.at[other],
                recv_sem=recv_sem.at[me],
                device_id={"stn": other // 2, "tm": other % 2},
                device_id_type=MESH,
            ).start()
        return carry

    lax.fori_loop(0, blocks, one_block, 0)
    own = pltpu.make_async_copy(send_buf.at[me], out_ref.at[me], own_sem)
    own.start()
    own.wait()
    for mask in range(1, group):
        other = flipped(me, mask, group)
        whole = pltpu.make_async_remote_copy(
            src_ref=send_buf.at[other],
            dst_ref=out_ref.at[other],
            send_sem=send_sem.at[other],
            recv_sem=recv_sem.at[other],
            device_id={"stn": other // 2, "tm": other % 2},
            device_id_type=MESH,
        )
        whole.wait_send()
        whole.wait_recv()


def correlate_kernel(in_ref, out_ref):
    stations, halves, blocks, _, pair, frames = in_ref.shape
    inputs = stations * blocks * ROWS
    step = pl.program_id(0)
    real = []
    imag = []
    for t in range(halves):
        both = in_ref[:, t, :, step].astype(jnp.float32)
        both = both.reshape(stations * blocks, pair, frames)
        real.append(both[:, :ROWS].reshape(inputs, frames))
        imag.append(both[:, ROWS:].reshape(inputs, frames))
    right = jnp.concatenate(real + imag, axis=1).astype(jnp.bfloat16)
    left = jnp.concatenate(imag + [-value for value in real], axis=1).astype(jnp.bfloat16)
    dims = (((1,), (1,)), ((), ()))
    left = jnp.concatenate([right, left], axis=0)
    product = lax.dot_general(left, right, dims, preferred_element_type=jnp.float32)
    out_ref[...] = product.reshape(2, inputs, inputs)


def kernel_shards(stations, halves, voltages, filter_taps):
    inputs_dev, sub_count, time_dev = voltages.shape
    taps_count, frame_len = filter_taps.shape
    frames = time_dev // frame_len
    group = stations * halves
    blocks = inputs_dev // ROWS
    keep = 16
    per_dev = frame_len // 2 // group
    share = np.float32(1.0 / math.sqrt(frames * halves))
    table = jnp.asarray(np.ascontiguousarray(transform_table(frame_len, frame_len // 2).T) * share)
    x = voltages.reshape(inputs_dev, sub_count, frames, frame_len)
    x = jnp.transpose(x, (0, 2, 1, 3)).reshape(inputs_dev, frames * sub_count, frame_len)
    rows = 2 * frame_len * ROWS // group
    vmem = pl.BlockSpec(memory_space=pltpu.VMEM)
    spectra = pl.pallas_call(
        functools.partial(spectra_kernel, group),
        out_shape=jax.ShapeDtypeStruct((group, blocks, rows, frames), jnp.bfloat16),
        in_specs=[pl.BlockSpec(memory_space=pl.ANY), vmem, vmem],
        out_specs=vmem,
        scratch_shapes=[
            pltpu.VMEM((inputs_dev, frames * 2, frame_len), jnp.int32),
            pltpu.VMEM((inputs_dev, keep * 2, frame_len), jnp.int32),
            pltpu.VMEM((2, keep + frames, frame_len), jnp.float32),
            pltpu.VMEM((2, frame_len * ROWS, frames), jnp.float32),
            pltpu.VMEM((group, blocks, rows, frames), jnp.bfloat16),
            pltpu.SemaphoreType.DMA((blocks,)),
            pltpu.SemaphoreType.DMA((blocks,)),
            pltpu.SemaphoreType.DMA((blocks,)),
            pltpu.SemaphoreType.DMA,
            pltpu.SemaphoreType.DMA((group,)),
            pltpu.SemaphoreType.DMA((group,)),
        ],
        compiler_params=pltpu.CompilerParams(
            collective_id=0, has_side_effects=True, vmem_limit_bytes=40960 * 1024
        ),
        name="spectra",
    )(x, filter_taps, table)
    spectra = spectra.reshape(stations, halves, blocks, sub_count * per_dev, 2 * ROWS, frames)
    inputs = stations * inputs_dev
    return pl.pallas_call(
        correlate_kernel,
        grid=(sub_count * per_dev,),
        out_shape=jax.ShapeDtypeStruct((2, sub_count, per_dev, inputs, inputs), jnp.float32),
        in_specs=[vmem],
        out_specs=pl.BlockSpec(
            (2, None, None, inputs, inputs), lambda s: (0, s // per_dev, s % per_dev, 0, 0)
        ),
        compiler_params=pltpu.CompilerParams(vmem_limit_bytes=40 * 1024 * 1024),
        name="correlate",
    )(spectra)


def shards(stations, halves, voltages, filter_taps):
    inputs_dev, sub_count, time_dev = voltages.shape
    taps_count, frame_len = filter_taps.shape
    group = stations * halves
    fits = (
        halves == 2
        and sub_count == 2
        and group & (group - 1) == 0
        and group <= 16
        and inputs_dev % ROWS == 0
        and frame_len == 128
        and time_dev == 128 * frame_len
        and taps_count == 16
    )
    if fits:
        return kernel_shards(stations, halves, voltages, filter_taps)
    return general_shards(voltages, filter_taps)


def solution(mesh):
    placed = (P("stn", "band", "tm"), P())
    return jax.shard_map(
        functools.partial(shards, mesh.shape["stn"], mesh.shape["tm"]),
        mesh=mesh,
        in_specs=placed,
        out_specs=P(None, None, ("band", "stn", "tm"), None, None),
        check_vma=False,
    )
```
